32 devices in a mesh: macro: 4 (over y, core), pool: 8 (over z, x).
Axes of the slice: x: 2, y: 2, z: 4, core: 2. Of those that a mesh axis runs over, the one named last changes fastest.
Arguments:
- panels: bfloat16 [8, 768, 768], P('pool', 'macro'), as said below
- loads: float32 [8, 9, 768], P('pool'), may hold values from -6 to 6
- family: int32 [2048, 1], P(('macro', 'pool')), may hold values from 0 to 7; in each aligned block of 64 rows (0 to 63, 64 to 127, ...) at most 8 rows name the same one
- contact: float32 [2048, 768], P(('macro', 'pool')), may hold values from 0.05 to 8
- strain: float32 [2048, 9], P(('macro', 'pool')), may hold values from -6 to 6
- previous: bfloat16 [2048, 6912], P(('macro', 'pool')), may hold values from -3 to 3
Outputs:
- fluct: bfloat16 [2048, 6912], P(('macro', 'pool'))
- stress: float32 [2048, 9], P(('macro', 'pool'))
- tangent: float32 [2048, 81], P(('macro', 'pool'))
The draws below stay inside these ranges and needn't reach their ends.
Inputs may be any that keep to these rules, and one draw needn't show every extreme that they name: Within the rows of one device no family is named more than 8 times, a bound that some block reaches. `panels`: each panel is symmetric and positive definite.
All inputs are finite; a program needn't handle non-finite values.
Results may differ from the reference program's by a relative error of at most 0.0085.
Values may be sent and summed in bfloat16 or wider, within the bound.
A program may use at most 64 MiB of HBM per device.

```python
import math
import jax
import jax.numpy as jnp
import numpy as np
from jax import lax

DOF = 768
RHS = 9
ITERS = 4
PT_DEV = 64
CAP = 8
FAMS = 8
POINTS = 2048


def draw_panels(key, part):
    yarn_width = 64
    yarn_index = jnp.arange(DOF, dtype=jnp.int32) // yarn_width
    coupled = (yarn_index[None, :] == yarn_index[:, None]) | (yarn_index[None, :] == yarn_index[:, None] + 1)
    factor = jax.random.normal(key, (FAMS, DOF, DOF), jnp.float32)
    factor = jnp.where(coupled[None, :, :], factor, 0.0)
    product_matrix = jnp.einsum('fik,fjk->fij', factor, factor, precision=lax.Precision.HIGHEST)
    product_matrix = 0.5 * (product_matrix + jnp.swapaxes(product_matrix, 1, 2))
    identity = jnp.eye(DOF, dtype=jnp.float32)
    matrix = product_matrix / (2.0 * yarn_width) + 0.2 * identity[None, :, :]
    return matrix.astype(jnp.bfloat16)


def steps_of(rng, shape, pieces, smallest, high):
    def one(axis_at, parts):
        draws = jax.random.uniform(jax.random.fold_in(jax.random.fold_in(rng, 6), axis_at), (parts,), jnp.float32, smallest / len(pieces), high / len(pieces))
        return jnp.repeat(jnp.exp(draws), shape[axis_at] // parts).reshape((-1,) + (1,) * (len(shape) - axis_at - 1))

    level = one(*pieces[0])
    for cut in pieces[1:]:
        level = level * one(*cut)
    return level


def deal_out(own_key, own, number, rows, amount, top, limit, slope):
    ranking = jax.random.permutation(own_key, amount)
    heavy_load, ordinary = shares(amount, rows * top, limit, slope, True), shares(amount, rows * top, limit, slope, False)
    places = jnp.arange(amount)

    def named(lengths, turn):
        used = int((lengths > 0).sum())
        fixed = max(1, used // 4)
        passed = fixed + (places - fixed + turn * (used - fixed)) % max(1, amount - fixed)
        return jnp.zeros((amount,), jnp.int32).at[ranking[jnp.where(places < fixed, places, passed)]].set(jnp.asarray(lengths, jnp.int32))

    lengths = jnp.where(number % 4 == 0, named(heavy_load, number // 4), named(ordinary, number - number // 4 - 1))
    mixed = jax.random.permutation(jax.random.fold_in(own, 3), amount)
    donor, sink = mixed[0:amount // 2 * 2:2], mixed[1:amount // 2 * 2:2]
    room = jnp.minimum(lengths[donor] - 1, limit - lengths[sink]) // 2
    room = jnp.where((donor == ranking[0]) | (sink == ranking[0]) | (lengths[sink] == 0), 0, jnp.maximum(room, 0))
    passed = jax.random.randint(jax.random.fold_in(own, 4), (amount // 2,), 0, 1 << 20) % (room + 1)
    lengths = lengths.at[donor].add(-passed).at[sink].add(passed)
    members = jnp.searchsorted(jnp.cumsum(lengths), jnp.arange(rows * top), side="right").astype(jnp.int32)
    listing = members.reshape(top, rows).T
    listing = listing[jax.random.permutation(jax.random.fold_in(own, 1), rows)]
    turn = jax.random.randint(jax.random.fold_in(own, 2), (rows, 1), 0, top)
    return jnp.take_along_axis(listing, (jnp.arange(top)[None, :] + turn) % top, axis=1)


def shares(number_of, total, limit, skew, full):
    weights = [(1 << 20) // math.isqrt(grade ** skew) + 1 for grade in range(1, number_of + 1)]
    largest = limit if full else min(limit, max(-(-total // number_of), total * weights[0] // sum(weights)))
    least = 1 if total - largest >= number_of - 1 else 0
    given, surplus = [largest] + [least] * (number_of - 1), total - largest - least * (number_of - 1)
    while surplus > 0:
        movable = [i for i in range(1, number_of) if given[i] < largest] or [i for i in range(1, number_of) if given[i] < limit]
        whole, budget = sum([weights[i] for i in movable]), surplus
        for i in movable:
            extra = min(limit - given[i], max(1, budget * weights[i] // whole), surplus)
            given[i] = given[i] + extra
            surplus = surplus - extra
    return np.array(given)


def bell_draw(rng, extent, scale, bound, pieces=(), kind=jnp.bfloat16):
    loudness = steps_of(rng, extent, pieces, -0.22, 0.18) if pieces else 1.0
    result = jax.random.normal(rng, extent, jnp.float32) * scale * loudness
    return jnp.minimum(jnp.maximum(result, -bound), bound).astype(kind)


def setup_inputs(seed: int = 0) -> dict:
    arg_keys = jax.random.split(jax.random.key(seed), 7)
    panels = draw_panels(jax.random.fold_in(arg_keys[6], 71), 0)
    loads = bell_draw(arg_keys[1], (FAMS, RHS, DOF), 1.0, 6.0, ((0, 8),), jnp.float32)
    family_keys = jax.random.split(jax.random.fold_in(arg_keys[2], 1), POINTS // PT_DEV)
    family_turns = jax.random.permutation(jax.random.fold_in(arg_keys[2], 3), POINTS // PT_DEV)
    family = jax.vmap(lambda own, number: deal_out(jax.random.fold_in(arg_keys[2], 2), own, number, PT_DEV, FAMS, 1, CAP, 2))(family_keys, family_turns).reshape((POINTS, 1))
    contact = jnp.clip(jnp.exp(math.log(8.0) - 5.075174 * jax.random.uniform(arg_keys[3], (POINTS, DOF), jnp.float32) ** steps_of(arg_keys[3], (POINTS, DOF), ((0, 32),), -0.2, 0.2)), 0.05, 8.0)
    strain = bell_draw(arg_keys[4], (POINTS, RHS), 1.0, 6.0, ((0, 32),), jnp.float32)
    previous = bell_draw(arg_keys[5], (POINTS, RHS * DOF), 0.5, 3.0, ((0, 32),))
    return {"panels": panels, "loads": loads, "family": family, "contact": contact, "strain": strain, "previous": previous}


def solve_cells(panel, load, contact_rows, previous_rows, strain_rows):
    cells = contact_rows.shape[0]
    width = panel.shape[0]
    count = load.shape[0]
    stiff = panel.astype(jnp.float32)
    inverse = 1.0 / jnp.diagonal(stiff)

    def apply_stiffness(field):
        flat = field.reshape(cells * count, width)
        product = jnp.dot(flat, stiff, precision=lax.Precision.HIGHEST).reshape(cells, count, width)
        return product + contact_rows[:, None, :] * field

    iterate = previous_rows.astype(jnp.float32).reshape(cells, count, width)
    residual = load[None, :, :] - apply_stiffness(iterate)
    scaled = inverse * residual
    direction = scaled
    current = jnp.sum(residual * scaled, axis=-1)
    for sweep in range(ITERS):
        image = apply_stiffness(direction)
        step_size = current / (jnp.sum(direction * image, axis=-1) + 1e-6)
        iterate = iterate + step_size[:, :, None] * direction
        residual = residual - step_size[:, :, None] * image
        scaled = inverse * residual
        updated = jnp.sum(residual * scaled, axis=-1)
        direction = scaled + (updated / (current + 1e-6))[:, :, None] * direction
        current = updated
    tangent = jnp.einsum("sik,jk->sij", iterate, load, precision=lax.Precision.HIGHEST) / width
    stress = jnp.einsum("sij,sj->si", tangent, strain_rows, precision=lax.Precision.HIGHEST)
    return (iterate.astype(jnp.bfloat16).reshape(cells, count * width), stress,
            tangent.reshape(cells, count * count))


def reference(panels, loads, family, contact, strain, previous):
    def one_point(inputs):
        member, contact_row, strain_row, previous_row = inputs
        panel = lax.dynamic_index_in_dim(panels, member, 0, keepdims=False)
        load = lax.dynamic_index_in_dim(loads, member, 0, keepdims=False)
        new_rows, stress_rows, tangent_rows = solve_cells(
            panel, load, contact_row[None, :], previous_row[None, :], strain_row[None, :])
        return new_rows[0], stress_rows[0], tangent_rows[0]

    fluct, stress, tangent = lax.map(one_point, (family[:, 0], contact, strain, previous))
    return fluct, stress, tangent
```

```python
import functools
import itertools
import math

import jax
import jax.numpy as jnp
from jax import lax
from jax.experimental import pallas as pl
from jax.experimental.pallas import tpu as pltpu
from jax.sharding import PartitionSpec as P

ITERS = 4
CAP = 8
LANES = 128
PACK = 16
CORES = 2
BF = jnp.bfloat16
F32 = jnp.float32


def split_pool(pool):
    fast = max(d for d in range(1, pool + 1) if pool % d == 0 and d * d <= pool)
    return pool // fast, fast


def half_plan(dof, macro):
    rows = dof // macro
    unit = math.gcd(rows, LANES)
    blocks = dof // LANES
    per = LANES // unit
    fixed = [(r, (r + k) % blocks) for r in range(blocks) for k in range((blocks - 1) // 2 + 1)]
    open_pairs = [(r, r + blocks // 2) for r in range(blocks // 2)] if blocks % 2 == 0 else []
    best = None
    for turned in itertools.product((0, 1), repeat=len(open_pairs)):
        chosen = fixed + [(b, a) if t else (a, b) for t, (a, b) in zip(turned, open_pairs)]
        lists = [[] for _ in range(macro)]
        for r, c in sorted(chosen):
            for q in range(per):
                stripe = r * per + q
                lists[stripe * unit // rows].append((stripe, c))
        most = max(len(each) for each in lists)
        if best is None or most < best[0]:
            best = (most, lists, chosen)
    return unit, best[0], best[1], [(r, c) for r, c in best[2] if r != c]


def by_distance(n):
    return [sorted(range(n), key=lambda s: (abs(s - p), s)) for p in range(n)]


def pick(table, at, k):
    out = jnp.int32(table[0][k])
    for p in range(1, len(table)):
        out = jnp.where(at == p, jnp.int32(table[p][k]), out)
    return out


def kernel(sizes, panel_ref, loads_ref, family_ref, contact_ref, strain_ref, previous_ref,
           fluct_ref, stress_ref, tangent_ref,
           held, whole, load, slot_prev, slot_contact, slot_strain, slot_out, slot_small,
           iterate, residual, direction, inverse_ref, send_sem, recv_sem):
    macro, pool, plan, cut = sizes
    unit, most, lists, mirrored = plan
    count, dof = loads_ref.shape[1], loads_ref.shape[2]
    rows = panel_ref.shape[1]
    points = family_ref.shape[0]
    slots = pool * CAP
    blocks = dof // LANES
    nz, nx = split_pool(pool)
    ny = macro // CORES
    total_rows = held.shape[2]
    cuts = ((0, cut), (cut, total_rows - cut))

    my_macro, my_pool = lax.axis_index("macro"), lax.axis_index("pool")
    pz, px = my_pool // nx, my_pool % nx
    py, pc = my_macro // CORES, my_macro % CORES
    here = (pz, px, py)
    extent = (nz, nx, ny)
    orders = tuple(by_distance(n) for n in extent)

    def device(at, core):
        z, x, y = at
        return (y * CORES + core, z * nx + x)

    def moved(axis, to):
        return tuple(to if a == axis else here[a] for a in range(3))

    barrier = pltpu.get_barrier_semaphore()
    pl.semaphore_signal(barrier, inc=1, device_id=device(here, 1 - pc), device_id_type=pl.DeviceIdType.MESH)
    expected = jnp.int32(1)
    for axis in range(3):
        for by in (-1, 1):
            to = here[axis] + by
            ok = jnp.logical_and(to >= 0, to < extent[axis])
            expected = expected + ok.astype(jnp.int32)

            @pl.when(ok)
            def _(axis=axis, to=to):
                pl.semaphore_signal(
                    barrier, inc=1, device_id=device(moved(axis, to), pc), device_id_type=pl.DeviceIdType.MESH)

    for m in range(macro):

        @pl.when(my_macro == m)
        def _(m=m):
            for t, (stripe, c) in enumerate(lists[m]):
                low = stripe * unit - m * rows
                held[m, my_pool, t * unit:(t + 1) * unit, :] = panel_ref[
                    0, low:low + unit, c * LANES:(c + 1) * LANES]
            for t, b in enumerate(range(m, blocks, macro)):
                part = loads_ref[0, :, b * LANES:(b + 1) * LANES]
                part = jnp.concatenate([part, jnp.zeros((PACK - count, LANES), F32)], axis=0)
                low = most * unit + t * PACK
                held[m, my_pool, low:low + PACK, :] = part.astype(BF)

    pl.semaphore_wait(barrier, expected)
    pending = []

    def copy_of(src, h, to, core, sem):
        m, p = src
        start, size = cuts[h]
        view = held.at[m, p, pl.ds(start, size), :]
        return pltpu.make_async_remote_copy(
            src_ref=view, dst_ref=view, send_sem=send_sem.at[sem], recv_sem=recv_sem.at[m, p, h],
            device_id=device(to, core), device_id_type=pl.DeviceIdType.MESH)

    def start(src, h, to, core, cond):
        copy = copy_of(src, h, to, core, len(pending))
        pending.append((copy, cond))
        if cond is None:
            copy.start()
        else:
            pl.when(cond)(copy.start)

    def arrive(src, h):
        copy_of(src, h, here, 1 - pc, 0).wait_recv()

    def along(src, h, axis, k, source):
        n, p = extent[axis], here[axis]
        if n == 1 or (k > 0 and n == 2):
            return
        if k == 0 and n == 2:
            start(src, h, moved(axis, 1 - p), pc, None)
        elif k == 0:
            for by in (1, -1):
                to = p + by
                start(src, h, moved(axis, to), pc, jnp.logical_and(to >= 0, to < n))
        else:
            to = jnp.where(p > source, p + 1, p - 1)
            start(src, h, moved(axis, to), pc, jnp.logical_and(to >= 0, to < n))

    paths = ((0, 1, 2), (0, 2, 1))

    def sources(ks):
        return tuple(here[a] if ks[a] == 0 else pick(orders[a], here[a], ks[a]) for a in range(3))

    def event(ks, h):
        at = sources(ks)
        src = device(at, pc)
        if any(ks):
            arrive(src, h)
        path = paths[h]
        last = max([i for i in range(3) if ks[path[i]]], default=0)
        for i in range(last, 3):
            along(src, h, path[i], ks[path[i]], at[path[i]])
        start(src, h, here, 1 - pc, None)

    def event_z(kz):
        for h in (0, 1):
            event((kz, 0, 0), h)

    def event_xy(kz):
        for k in range(1, nx):
            event((kz, k, 0), 0)
        for k in range(1, ny):
            event((kz, 0, k), 1)
        for kx in range(nx):
            for ky in range(1, ny):
                event((kz, kx, ky), 0)
        for ky in range(ny):
            for kx in range(1, nx):
                event((kz, kx, ky), 1)

    def sibling(kz):
        for kx in range(nx):
            for ky in range(ny):
                at = sources((kz, kx, ky))
                for h in (0, 1):
                    arrive(device(at, 1 - pc), h)

    event_z(0)

    family = family_ref[...]
    named = family == lax.broadcasted_iota(jnp.int32, (points, pool), 1)
    row_at = lax.broadcasted_iota(jnp.int32, (points, points), 0)
    col_at = lax.broadcasted_iota(jnp.int32, (points, points), 1)
    before = jnp.dot((col_at < row_at).astype(BF), named.astype(BF), preferred_element_type=F32)
    rank = jnp.sum(jnp.where(named, before, 0.0), axis=1, keepdims=True)
    slot = family * CAP + rank.astype(jnp.int32)
    slot_row = jnp.sum(jnp.where(row_at == col_at, slot.astype(F32), 0.0), axis=0, keepdims=True).astype(jnp.int32)
    placing = (lax.broadcasted_iota(jnp.int32, (slots, points), 0) == slot_row).astype(BF)
    taking = (slot == lax.broadcasted_iota(jnp.int32, (points, slots), 1)).astype(BF)

    def parts3(value):
        high = value.astype(BF)
        rest = value - high.astype(F32)
        middle = rest.astype(BF)
        return high, middle, (rest - middle.astype(F32)).astype(BF)

    def move3(matrix, value):
        return sum(jnp.dot(matrix, part, preferred_element_type=F32) for part in parts3(value))

    for i in range(count):
        span = slice(i * dof, (i + 1) * dof)
        slot_prev[:, span] = jnp.dot(placing, previous_ref[:, span], preferred_element_type=F32).astype(BF)
    slot_contact[...] = move3(placing, contact_ref[...])
    slot_strain[...] = move3(placing, strain_ref[...])

    eye = (lax.broadcasted_iota(jnp.int32, (LANES, LANES), 0)
           == lax.broadcasted_iota(jnp.int32, (LANES, LANES), 1))

    def assemble(j, f):
        for m in range(macro):
            for t, (stripe, c) in enumerate(lists[m]):
                whole[j, stripe * unit:(stripe + 1) * unit, c * LANES:(c + 1) * LANES] = held[
                    m, f, t * unit:(t + 1) * unit, :]
            for t, b in enumerate(range(m, blocks, macro)):
                low = most * unit + t * PACK
                load[j, :, b * LANES:(b + 1) * LANES] = held[m, f, low:low + PACK, :]
        for r, c in mirrored:
            block = whole[j, r * LANES:(r + 1) * LANES, c * LANES:(c + 1) * LANES]
            whole[j, c * LANES:(c + 1) * LANES, r * LANES:(r + 1) * LANES] = block.T
        for r in range(blocks):
            span = slice(r * LANES, (r + 1) * LANES)
            diagonal = jnp.sum(jnp.where(eye, whole[j, span, span].astype(F32), 0.0), axis=0, keepdims=True)
            inverse_ref[j, :, span] = 1.0 / diagonal

    def solve_pair(pair):
        at16 = pl.ds(pl.multiple_of(pair * 2 * CAP, 2 * CAP), 2 * CAP)
        for j in (0, 1):
            assemble(j, pair * 2 + j)
        for i in range(count):
            both = slot_prev[at16, i * dof:(i + 1) * dof].astype(F32)
            iterate[0, i * CAP:(i + 1) * CAP, :] = both[:CAP]
            iterate[1, i * CAP:(i + 1) * CAP, :] = both[CAP:]

        def contact_of(j):
            return slot_contact[pl.ds(pl.multiple_of(pair * 2 * CAP + j * CAP, CAP), CAP), :]

        def apply(j, field):
            product = jnp.dot(field.astype(BF), whole[j], preferred_element_type=F32)
            extra = contact_of(j)[None, :, :] * field.reshape(count, CAP, dof)
            return product + extra.reshape(count * CAP, dof)

        current = []
        for j in (0, 1):
            loads = load[j, 0:count, :].astype(F32)
            wide = jnp.broadcast_to(loads[:, None, :], (count, CAP, dof)).reshape(count * CAP, dof)
            left = wide - apply(j, iterate[j])
            scaled = inverse_ref[j] * left
            residual[j] = left
            direction[j] = scaled
            current.append(jnp.sum(left * scaled, axis=-1, keepdims=True))

        def sweep(_, current):
            after = []
            for j in (0, 1):
                toward = direction[j]
                image = apply(j, toward)
                step = current[j] / (jnp.sum(toward * image, axis=-1, keepdims=True) + 1e-6)
                iterate[j] = iterate[j] + step * toward
                left = residual[j] - step * image
                scaled = inverse_ref[j] * left
                updated = jnp.sum(left * scaled, axis=-1, keepdims=True)
                residual[j] = left
                direction[j] = scaled + (updated / (current[j] + 1e-6)) * toward
                after.append(updated)
            return tuple(after)

        lax.fori_loop(0, ITERS, sweep, tuple(current))

        for i in range(count):
            span = slice(i * CAP, (i + 1) * CAP)
            both = jnp.concatenate([iterate[0, span, :], iterate[1, span, :]], axis=0)
            slot_out[at16, i * dof:(i + 1) * dof] = both.astype(BF)
        for j in (0, 1):
            mine = pl.ds(pl.multiple_of(pair * 2 * CAP + j * CAP, CAP), CAP)
            value = iterate[j]
            high = value.astype(BF)
            low = (value - high.astype(F32)).astype(BF)
            weights = load[j]
            contract = (((1,), (1,)), ((), ()))
            tang = (lax.dot_general(high, weights, contract, preferred_element_type=F32)
                    + lax.dot_general(low, weights, contract, preferred_element_type=F32)) * (1.0 / dof)
            strain = slot_strain[mine, :]
            for i in range(count):
                piece = tang[i * CAP:(i + 1) * CAP, 0:count]
                slot_small[mine, i * count:(i + 1) * count] = piece
                slot_small[mine, count * count + i:count * count + i + 1] = jnp.sum(
                    piece * strain, axis=-1, keepdims=True)

    def solve(kz):
        at = pick(orders[0], pz, kz) if kz else pz
        for q in range(nx // 2):
            solve_pair(at * (nx // 2) + q)

    for kz in range(nz):
        if kz + 1 < nz:
            event_z(kz + 1)
        event_xy(kz)
        sibling(kz)
        solve(kz)

    for i in range(count):
        span = slice(i * dof, (i + 1) * dof)
        fluct_ref[:, span] = jnp.dot(taking, slot_out[:, span], preferred_element_type=F32).astype(BF)
    small = move3(taking, slot_small[...])
    tangent_ref[...] = small[:, 0:count * count]
    stress_ref[...] = small[:, count * count:count * count + count]

    for copy, cond in pending:
        if cond is None:
            copy.wait_send()
        else:
            pl.when(cond)(copy.wait_send)


def count_sends(nz, nx, ny):
    def along(n, k):
        if n == 1 or (k > 0 and n == 2):
            return 0
        return 1 if n == 2 or k > 0 else 2

    total = 0
    for path in ((0, 1, 2), (0, 2, 1)):
        for ks in itertools.product(range(nz), range(nx), range(ny)):
            last = max([i for i in range(3) if ks[path[i]]], default=0)
            total += 1 + sum(along((nz, nx, ny)[path[i]], ks[path[i]]) for i in range(last, 3))
    return total


def on_device(macro, pool, panels, loads, family, contact, strain, previous):
    points, dof = contact.shape
    count = strain.shape[1]
    plan = half_plan(dof, macro)
    unit, most = plan[0], plan[1]
    shares = -(-(dof // LANES) // macro)
    total_rows = most * unit + shares * PACK
    cut = -(-total_rows // (2 * PACK)) * PACK
    slots = pool * CAP
    nz, nx = split_pool(pool)
    vmem = pl.BlockSpec(memory_space=pltpu.VMEM)
    return pl.pallas_call(
        functools.partial(kernel, (macro, pool, plan, cut)),
        out_shape=(
            jax.ShapeDtypeStruct(previous.shape, BF),
            jax.ShapeDtypeStruct((points, count), F32),
            jax.ShapeDtypeStruct((points, count * count), F32),
        ),
        in_specs=[vmem] * 6,
        out_specs=(vmem,) * 3,
        scratch_shapes=[
            pltpu.VMEM((macro, pool, total_rows, LANES), BF),
            pltpu.VMEM((2, dof, dof), BF),
            pltpu.VMEM((2, PACK, dof), BF),
            pltpu.VMEM((slots, count * dof), BF),
            pltpu.VMEM((slots, dof), F32),
            pltpu.VMEM((slots, count), F32),
            pltpu.VMEM((slots, count * dof), BF),
            pltpu.VMEM((slots, LANES), F32),
            pltpu.VMEM((2, count * CAP, dof), F32),
            pltpu.VMEM((2, count * CAP, dof), F32),
            pltpu.VMEM((2, count * CAP, dof), F32),
            pltpu.VMEM((2, 1, dof), F32),
            pltpu.SemaphoreType.DMA((count_sends(nz, nx, macro // CORES),)),
            pltpu.SemaphoreType.DMA((macro, pool, 2)),
        ],
        compiler_params=pltpu.CompilerParams(
            collective_id=0, has_side_effects=True, vmem_limit_bytes=56 * 1024 * 1024),
    )(panels, loads, family, contact, strain, previous)


def solution(mesh):
    placed = (
        P("pool", "macro", None),
        P("pool", None, None),
        P(("macro", "pool"), None),
        P(("macro", "pool"), None),
        P(("macro", "pool"), None),
        P(("macro", "pool"), None),
    )
    return jax.shard_map(
        functools.partial(on_device, mesh.shape["macro"], mesh.shape["pool"]),
        mesh=mesh,
        in_specs=placed,
        out_specs=(
            P(("macro", "pool"), None),
            P(("macro", "pool"), None),
            P(("macro", "pool"), None),
        ),
        check_vma=False,
    )
```

```python
import functools
import itertools
import math

import jax
import jax.numpy as jnp
from jax import lax
from jax.experimental import pallas as pl
from jax.experimental.pallas import tpu as pltpu
from jax.sharding import PartitionSpec as P

ITERS = 4
CAP = 8
LANES = 128
PACK = 16
CORES = 2
BF = jnp.bfloat16
F32 = jnp.float32


def split_pool(pool):
    fast = max(d for d in range(1, pool + 1) if pool % d == 0 and d * d <= pool)
    return pool // fast, fast


def half_plan(dof, macro):
    rows = dof // macro
    unit = math.gcd(rows, LANES)
    blocks = dof // LANES
    per = LANES // unit
    fixed = [(r, (r + k) % blocks) for r in range(blocks) for k in range((blocks - 1) // 2 + 1)]
    open_pairs = [(r, r + blocks // 2) for r in range(blocks // 2)] if blocks % 2 == 0 else []
    best = None
    for turned in itertools.product((0, 1), repeat=len(open_pairs)):
        chosen = fixed + [(b, a) if t else (a, b) for t, (a, b) in zip(turned, open_pairs)]
        lists = [[] for _ in range(macro)]
        for r, c in sorted(chosen):
            for q in range(per):
                stripe = r * per + q
                lists[stripe * unit // rows].append((stripe, c))
        most = max(len(each) for each in lists)
        if best is None or most < best[0]:
            best = (most, lists, chosen)
    return unit, best[0], best[1], [(r, c) for r, c in best[2] if r != c]


def by_distance(n):
    return [sorted(range(n), key=lambda s: (abs(s - p), s)) for p in range(n)]


def pick(table, at, k):
    out = jnp.int32(table[0][k])
    for p in range(1, len(table)):
        out = jnp.where(at == p, jnp.int32(table[p][k]), out)
    return out


NT = (((1,), (1,)), ((), ()))


def parts3(value):
    high = value.astype(BF)
    rest = value - high.astype(F32)
    middle = rest.astype(BF)
    return high, middle, (rest - middle.astype(F32)).astype(BF)


def slots_of(family_row, pool):
    points = family_row.shape[1]
    row_at = lax.broadcasted_iota(jnp.int32, (points, points), 0)
    col_at = lax.broadcasted_iota(jnp.int32, (points, points), 1)
    eye = row_at == col_at
    wide = jnp.broadcast_to(family_row.astype(F32), (points, points))
    family = jnp.sum(jnp.where(eye, wide, 0.0), axis=1, keepdims=True).astype(jnp.int32)
    earlier = jnp.logical_and(wide.astype(jnp.int32) == family, col_at < row_at)
    rank = jnp.sum(jnp.where(earlier, 1.0, 0.0), axis=1, keepdims=True)
    slot = family * CAP + rank.astype(jnp.int32)
    slot_row = jnp.sum(jnp.where(eye, slot.astype(F32), 0.0), axis=0, keepdims=True).astype(jnp.int32)
    return slot, slot_row


def unplace_kernel(pool, count, family_ref, out_ref, small_ref, fluct_ref, stress_ref, tangent_ref):
    points = family_ref.shape[1]
    slot, _ = slots_of(family_ref[...], pool)
    taking = (slot == lax.broadcasted_iota(jnp.int32, (points, pool * CAP), 1)).astype(BF)
    fluct_ref[...] = jnp.dot(taking, out_ref[...], preferred_element_type=F32).astype(BF)

    @pl.when(pl.program_id(0) == 0)
    def _():
        small = sum(jnp.dot(taking, part, preferred_element_type=F32) for part in parts3(small_ref[...]))
        tangent_ref[...] = small[:, 0:count * count]
        at = lax.broadcasted_iota(jnp.int32, (PACK, LANES), 0) + count * count
        picking = (at == lax.broadcasted_iota(jnp.int32, (PACK, LANES), 1)).astype(BF)
        turned = sum(lax.dot_general(picking, part, NT, preferred_element_type=F32) for part in parts3(small))
        stress_ref[...] = turned[0:count, :]


def kernel(sizes, panel_ref, loads_ref, family_ref, contact_ref, strain_ref, previous_ref,
           slot_out, slot_small,
           held, whole, load, slot_prev, slot_contact, slot_strain,
           iterate, residual, direction, inverse_ref, send_sem, recv_sem):
    macro, pool, plan, cut = sizes
    unit, most, lists, mirrored = plan
    count, dof = loads_ref.shape[0], loads_ref.shape[2]
    rows = panel_ref.shape[1]
    points = family_ref.shape[1]
    slots = pool * CAP
    blocks = dof // LANES
    nz, nx = split_pool(pool)
    ny = macro // CORES
    total_rows = held.shape[2]
    cuts = ((0, cut), (cut, total_rows - cut))

    my_macro, my_pool = lax.axis_index("macro"), lax.axis_index("pool")
    pz, px = my_pool // nx, my_pool % nx
    py, pc = my_macro // CORES, my_macro % CORES
    here = (pz, px, py)
    extent = (nz, nx, ny)
    orders = tuple(by_distance(n) for n in extent)

    def device(at, core):
        z, x, y = at
        return (y * CORES + core, z * nx + x)

    def moved(axis, to):
        return tuple(to if a == axis else here[a] for a in range(3))

    barrier = pltpu.get_barrier_semaphore()
    pl.semaphore_signal(barrier, inc=1, device_id=device(here, 1 - pc), device_id_type=pl.DeviceIdType.MESH)
    expected = jnp.int32(1)
    for axis in range(3):
        for by in (-1, 1):
            to = here[axis] + by
            ok = jnp.logical_and(to >= 0, to < extent[axis])
            expected = expected + ok.astype(jnp.int32)

            @pl.when(ok)
            def _(axis=axis, to=to):
                pl.semaphore_signal(
                    barrier, inc=1, device_id=device(moved(axis, to), pc), device_id_type=pl.DeviceIdType.MESH)

    for m in range(macro):

        @pl.when(my_macro == m)
        def _(m=m):
            for t, (stripe, c) in enumerate(lists[m]):
                low = stripe * unit - m * rows
                held[m, my_pool, t * unit:(t + 1) * unit, :] = panel_ref[
                    0, low:low + unit, c * LANES:(c + 1) * LANES]
            for t, b in enumerate(range(m, blocks, macro)):
                part = loads_ref[:, 0, b * LANES:(b + 1) * LANES]
                part = jnp.concatenate([part, jnp.zeros((PACK - count, LANES), F32)], axis=0)
                low = most * unit + t * PACK
                held[m, my_pool, low:low + PACK, :] = part.astype(BF)

    pl.semaphore_wait(barrier, expected)
    pending = []

    def copy_of(src, h, to, core, sem):
        m, p = src
        start, size = cuts[h]
        view = held.at[m, p, pl.ds(start, size), :]
        return pltpu.make_async_remote_copy(
            src_ref=view, dst_ref=view, send_sem=send_sem.at[sem], recv_sem=recv_sem.at[m, p, h],
            device_id=device(to, core), device_id_type=pl.DeviceIdType.MESH)

    def start(src, h, to, core, cond):
        copy = copy_of(src, h, to, core, len(pending))
        pending.append((copy, cond))
        if cond is None:
            copy.start()
        else:
            pl.when(cond)(copy.start)

    def arrive(src, h):
        copy_of(src, h, here, 1 - pc, 0).wait_recv()

    def along(src, h, axis, k, source):
        n, p = extent[axis], here[axis]
        if n == 1 or (k > 0 and n == 2):
            return
        if k == 0 and n == 2:
            start(src, h, moved(axis, 1 - p), pc, None)
        elif k == 0:
            for by in (1, -1):
                to = p + by
                start(src, h, moved(axis, to), pc, jnp.logical_and(to >= 0, to < n))
        else:
            to = jnp.where(p > source, p + 1, p - 1)
            start(src, h, moved(axis, to), pc, jnp.logical_and(to >= 0, to < n))

    paths = ((0, 1, 2), (0, 2, 1))

    def sources(ks):
        return tuple(here[a] if ks[a] == 0 else pick(orders[a], here[a], ks[a]) for a in range(3))

    def event(ks, h):
        at = sources(ks)
        src = device(at, pc)
        if any(ks):
            arrive(src, h)
        path = paths[h]
        last = max([i for i in range(3) if ks[path[i]]], default=0)
        for i in range(last, 3):
            along(src, h, path[i], ks[path[i]], at[path[i]])
        start(src, h, here, 1 - pc, None)

    def events_z(kz):
        return [functools.partial(event, (kz, 0, 0), h) for h in (0, 1)] if kz < nz else []

    def events_xy(kz):
        if kz >= nz:
            return []
        first = [((kz, k, 0), 0) for k in range(1, nx)] + [((kz, 0, k), 1) for k in range(1, ny)]
        second = [((kz, kx, ky), 0) for kx in range(nx) for ky in range(1, ny)]
        second += [((kz, kx, ky), 1) for ky in range(ny) for kx in range(1, nx)]
        return [functools.partial(event, ks, h) for ks, h in dict.fromkeys(first + second)]

    def run(steps):
        for step in steps:
            step()

    def sibling(kz):
        for kx in range(nx):
            for ky in range(ny):
                at = sources((kz, kx, ky))
                for h in (0, 1):
                    arrive(device(at, 1 - pc), h)

    run(events_z(0))

    _, slot_row = slots_of(family_ref[...], pool)
    placing = (lax.broadcasted_iota(jnp.int32, (slots, points), 0) == slot_row).astype(BF)

    for i in range(count):
        span = slice(i * dof, (i + 1) * dof)
        slot_prev[:, span] = jnp.dot(placing, previous_ref[:, span], preferred_element_type=F32).astype(BF)
    slot_contact[...] = sum(
        jnp.dot(placing, part, preferred_element_type=F32) for part in parts3(contact_ref[...]))
    slot_strain[...] = sum(
        lax.dot_general(placing, part, NT, preferred_element_type=F32) for part in parts3(strain_ref[...]))
    slot_small[...] = jnp.zeros_like(slot_small)

    eye = (lax.broadcasted_iota(jnp.int32, (LANES, LANES), 0)
           == lax.broadcasted_iota(jnp.int32, (LANES, LANES), 1))

    def assemble(j, f):
        for m in range(macro):
            for t, (stripe, c) in enumerate(lists[m]):
                whole[j, stripe * unit:(stripe + 1) * unit, c * LANES:(c + 1) * LANES] = held[
                    m, f, t * unit:(t + 1) * unit, :]
            for t, b in enumerate(range(m, blocks, macro)):
                low = most * unit + t * PACK
                load[j, :, b * LANES:(b + 1) * LANES] = held[m, f, low:low + PACK, :]
        for r, c in mirrored:
            block = whole[j, r * LANES:(r + 1) * LANES, c * LANES:(c + 1) * LANES]
            whole[j, c * LANES:(c + 1) * LANES, r * LANES:(r + 1) * LANES] = block.T
        for r in range(blocks):
            span = slice(r * LANES, (r + 1) * LANES)
            diagonal = jnp.sum(jnp.where(eye, whole[j, span, span].astype(F32), 0.0), axis=0, keepdims=True)
            inverse_ref[j, :, span] = 1.0 / diagonal

    def solve_pair(pair, between):
        at16 = pl.ds(pl.multiple_of(pair * 2 * CAP, 2 * CAP), 2 * CAP)
        for j in (0, 1):
            assemble(j, pair * 2 + j)
        for i in range(count):
            both = slot_prev[at16, i * dof:(i + 1) * dof].astype(F32)
            iterate[0, i * CAP:(i + 1) * CAP, :] = both[:CAP]
            iterate[1, i * CAP:(i + 1) * CAP, :] = both[CAP:]

        def contact_of(j):
            return slot_contact[pl.ds(pl.multiple_of(pair * 2 * CAP + j * CAP, CAP), CAP), :]

        def apply(j, field):
            product = jnp.dot(field.astype(BF), whole[j], preferred_element_type=F32)
            extra = contact_of(j)[None, :, :] * field.reshape(count, CAP, dof)
            return product + extra.reshape(count * CAP, dof)

        current = []
        for j in (0, 1):
            loads = load[j, 0:count, :].astype(F32)
            wide = jnp.broadcast_to(loads[:, None, :], (count, CAP, dof)).reshape(count * CAP, dof)
            left = wide - apply(j, iterate[j])
            scaled = inverse_ref[j] * left
            residual[j] = left
            direction[j] = scaled
            current.append(jnp.sum(left * scaled, axis=-1, keepdims=True))

        def sweep(current):
            after = []
            for j in (0, 1):
                toward = direction[j]
                image = apply(j, toward)
                step = current[j] / (jnp.sum(toward * image, axis=-1, keepdims=True) + 1e-6)
                iterate[j] = iterate[j] + step * toward
                left = residual[j] - step * image
                scaled = inverse_ref[j] * left
                updated = jnp.sum(left * scaled, axis=-1, keepdims=True)
                residual[j] = left
                direction[j] = scaled + (updated / (current[j] + 1e-6)) * toward
                after.append(updated)
            return after

        between()
        for _ in range(ITERS):
            current = sweep(current)
            between()

        for i in range(count):
            span = slice(i * CAP, (i + 1) * CAP)
            both = jnp.concatenate([iterate[0, span, :], iterate[1, span, :]], axis=0)
            slot_out[at16, i * dof:(i + 1) * dof] = both.astype(BF)
        for j in (0, 1):
            mine = pl.ds(pl.multiple_of(pair * 2 * CAP + j * CAP, CAP), CAP)
            value = iterate[j]
            high = value.astype(BF)
            low = (value - high.astype(F32)).astype(BF)
            weights = load[j]
            tang = (lax.dot_general(high, weights, NT, preferred_element_type=F32)
                    + lax.dot_general(low, weights, NT, preferred_element_type=F32)) * (1.0 / dof)
            strain = slot_strain[mine, :]
            for i in range(count):
                piece = tang[i * CAP:(i + 1) * CAP, 0:count]
                slot_small[mine, i * count:(i + 1) * count] = piece
                slot_small[mine, count * count + i:count * count + i + 1] = jnp.sum(
                    piece * strain, axis=-1, keepdims=True)

    def solve(kz, steps):
        at = pick(orders[0], pz, kz) if kz else pz
        share = -(-len(steps) // (ITERS + 1))

        def between():
            run(steps[:share])
            del steps[:share]

        for q in range(nx // 2):
            solve_pair(at * (nx // 2) + q, between)

    run(events_z(1) + events_xy(0) + events_z(2))
    for kz in range(nz):
        sibling(kz)
        solve(kz, events_z(kz + 3) + events_xy(kz + 1))

    for copy, cond in pending:
        if cond is None:
            copy.wait_send()
        else:
            pl.when(cond)(copy.wait_send)


def count_sends(nz, nx, ny):
    def along(n, k):
        if n == 1 or (k > 0 and n == 2):
            return 0
        return 1 if n == 2 or k > 0 else 2

    total = 0
    for path in ((0, 1, 2), (0, 2, 1)):
        for ks in itertools.product(range(nz), range(nx), range(ny)):
            last = max([i for i in range(3) if ks[path[i]]], default=0)
            total += 1 + sum(along((nz, nx, ny)[path[i]], ks[path[i]]) for i in range(last, 3))
    return total


def on_device(macro, pool, panels, loads, family, contact, strain, previous):
    points, dof = contact.shape
    count = strain.shape[1]
    plan = half_plan(dof, macro)
    unit, most = plan[0], plan[1]
    shares = -(-(dof // LANES) // macro)
    total_rows = most * unit + shares * PACK
    cut = -(-total_rows // (2 * PACK)) * PACK
    slots = pool * CAP
    nz, nx = split_pool(pool)
    vmem = pl.BlockSpec(memory_space=pltpu.VMEM)
    family_row = family.T
    slot_out, slot_small = pl.pallas_call(
        functools.partial(kernel, (macro, pool, plan, cut)),
        out_shape=(
            jax.ShapeDtypeStruct((slots, count * dof), BF),
            jax.ShapeDtypeStruct((slots, LANES), F32),
        ),
        in_specs=[vmem] * 6,
        out_specs=(vmem,) * 2,
        scratch_shapes=[
            pltpu.VMEM((macro, pool, total_rows, LANES), BF),
            pltpu.VMEM((2, dof, dof), BF),
            pltpu.VMEM((2, PACK, dof), BF),
            pltpu.VMEM((slots, count * dof), BF),
            pltpu.VMEM((slots, dof), F32),
            pltpu.VMEM((slots, count), F32),
            pltpu.VMEM((2, count * CAP, dof), F32),
            pltpu.VMEM((2, count * CAP, dof), F32),
            pltpu.VMEM((2, count * CAP, dof), F32),
            pltpu.VMEM((2, 1, dof), F32),
            pltpu.SemaphoreType.DMA((count_sends(nz, nx, macro // CORES),)),
            pltpu.SemaphoreType.DMA((macro, pool, 2)),
        ],
        compiler_params=pltpu.CompilerParams(
            collective_id=0, has_side_effects=True, vmem_limit_bytes=56 * 1024 * 1024),
    )(panels, loads.transpose(1, 0, 2), family_row, contact, strain.T, previous)
    fluct, stress, tangent = pl.pallas_call(
        functools.partial(unplace_kernel, pool, count),
        grid=(count,),
        out_shape=(
            jax.ShapeDtypeStruct(previous.shape, BF),
            jax.ShapeDtypeStruct((count, points), F32),
            jax.ShapeDtypeStruct((points, count * count), F32),
        ),
        in_specs=[
            pl.BlockSpec((1, points), lambda i: (0, 0)),
            pl.BlockSpec((slots, dof), lambda i: (0, i)),
            pl.BlockSpec((slots, LANES), lambda i: (0, 0)),
        ],
        out_specs=(
            pl.BlockSpec((points, dof), lambda i: (0, i)),
            pl.BlockSpec((count, points), lambda i: (0, 0)),
            pl.BlockSpec((points, count * count), lambda i: (0, 0)),
        ),
    )(family_row, slot_out, slot_small)
    return fluct, stress.T, tangent


def solution(mesh):
    placed = (
        P("pool", "macro", None),
        P("pool", None, None),
        P(("macro", "pool"), None),
        P(("macro", "pool"), None),
        P(("macro", "pool"), None),
        P(("macro", "pool"), None),
    )
    return jax.shard_map(
        functools.partial(on_device, mesh.shape["macro"], mesh.shape["pool"]),
        mesh=mesh,
        in_specs=placed,
        out_specs=(
            P(("macro", "pool"), None),
            P(("macro", "pool"), None),
            P(("macro", "pool"), None),
        ),
        check_vma=False,
    )
```

```python
import functools
import itertools
import math

import jax
import jax.numpy as jnp
from jax import lax
from jax.experimental import pallas as pl
from jax.experimental.pallas import tpu as pltpu
from jax.sharding import PartitionSpec as P

ITERS = 4
CAP = 8
LANES = 128
PACK = 16
CORES = 2
BF = jnp.bfloat16
F32 = jnp.float32


def split_pool(pool):
    fast = max(d for d in range(1, pool + 1) if pool % d == 0 and d * d <= pool)
    return pool // fast, fast


def half_plan(dof, macro):
    rows = dof // macro
    unit = math.gcd(rows, LANES)
    blocks = dof // LANES
    per = LANES // unit
    fixed = [(r, (r + k) % blocks) for r in range(blocks) for k in range((blocks - 1) // 2 + 1)]
    open_pairs = [(r, r + blocks // 2) for r in range(blocks // 2)] if blocks % 2 == 0 else []
    best = None
    for turned in itertools.product((0, 1), repeat=len(open_pairs)):
        chosen = fixed + [(b, a) if t else (a, b) for t, (a, b) in zip(turned, open_pairs)]
        lists = [[] for _ in range(macro)]
        for r, c in sorted(chosen):
            for q in range(per):
                stripe = r * per + q
                lists[stripe * unit // rows].append((stripe, c))
        most = max(len(each) for each in lists)
        if best is None or most < best[0]:
            best = (most, lists, chosen)
    return unit, best[0], best[1], [(r, c) for r, c in best[2] if r != c]


def by_distance(n):
    return [sorted(range(n), key=lambda s: (abs(s - p), s)) for p in range(n)]


def pick(table, at, k):
    out = jnp.int32(table[0][k])
    for p in range(1, len(table)):
        out = jnp.where(at == p, jnp.int32(table[p][k]), out)
    return out


NT = (((1,), (1,)), ((), ()))


def parts3(value):
    high = value.astype(BF)
    rest = value - high.astype(F32)
    middle = rest.astype(BF)
    return high, middle, (rest - middle.astype(F32)).astype(BF)


def slots_of(family_row, pool):
    points = family_row.shape[1]
    row_at = lax.broadcasted_iota(jnp.int32, (points, points), 0)
    col_at = lax.broadcasted_iota(jnp.int32, (points, points), 1)
    eye = row_at == col_at
    wide = jnp.broadcast_to(family_row.astype(F32), (points, points))
    family = jnp.sum(jnp.where(eye, wide, 0.0), axis=1, keepdims=True).astype(jnp.int32)
    earlier = jnp.logical_and(wide.astype(jnp.int32) == family, col_at < row_at)
    rank = jnp.sum(jnp.where(earlier, 1.0, 0.0), axis=1, keepdims=True)
    slot = family * CAP + rank.astype(jnp.int32)
    slot_row = jnp.sum(jnp.where(eye, slot.astype(F32), 0.0), axis=0, keepdims=True).astype(jnp.int32)
    return slot, slot_row


def unplace_kernel(pool, count, family_ref, out_ref, small_ref, fluct_ref, stress_ref, tangent_ref):
    points = family_ref.shape[1]
    slot, _ = slots_of(family_ref[...], pool)
    taking = (slot == lax.broadcasted_iota(jnp.int32, (points, pool * CAP), 1)).astype(BF)
    fluct_ref[...] = jnp.dot(taking, out_ref[...], preferred_element_type=F32).astype(BF)
    small = sum(jnp.dot(taking, part, preferred_element_type=F32) for part in parts3(small_ref[...]))
    tangent_ref[...] = small[:, 0:count * count]
    at = lax.broadcasted_iota(jnp.int32, (PACK, LANES), 0) + count * count
    picking = (at == lax.broadcasted_iota(jnp.int32, (PACK, LANES), 1)).astype(BF)
    turned = sum(lax.dot_general(picking, part, NT, preferred_element_type=F32) for part in parts3(small))
    stress_ref[...] = turned[0:count, :]


def kernel(sizes, panel_ref, loads_ref, family_ref, contact_ref, strain_ref, previous_ref,
           slot_out, slot_small,
           held, whole, load, slot_prev, slot_contact, slot_strain,
           iterate, residual, direction, product, inverse_ref, send_sem, recv_sem):
    macro, pool, plan, cut = sizes
    unit, most, lists, mirrored = plan
    count, dof = loads_ref.shape[0], loads_ref.shape[2]
    rows = panel_ref.shape[1]
    points = family_ref.shape[1]
    slots = pool * CAP
    blocks = dof // LANES
    nz, nx = split_pool(pool)
    ny = macro // CORES
    total_rows = held.shape[2]
    cuts = ((0, cut), (cut, total_rows - cut))

    my_macro, my_pool = lax.axis_index("macro"), lax.axis_index("pool")
    pz, px = my_pool // nx, my_pool % nx
    py, pc = my_macro // CORES, my_macro % CORES
    here = (pz, px, py)
    extent = (nz, nx, ny)
    orders = tuple(by_distance(n) for n in extent)

    def device(at, core):
        z, x, y = at
        return (y * CORES + core, z * nx + x)

    def moved(axis, to):
        return tuple(to if a == axis else here[a] for a in range(3))

    barrier = pltpu.get_barrier_semaphore()
    pl.semaphore_signal(barrier, inc=1, device_id=device(here, 1 - pc), device_id_type=pl.DeviceIdType.MESH)
    expected = jnp.int32(1)
    for axis in range(3):
        for by in (-1, 1):
            to = here[axis] + by
            ok = jnp.logical_and(to >= 0, to < extent[axis])
            expected = expected + ok.astype(jnp.int32)

            @pl.when(ok)
            def _(axis=axis, to=to):
                pl.semaphore_signal(
                    barrier, inc=1, device_id=device(moved(axis, to), pc), device_id_type=pl.DeviceIdType.MESH)

    for m in range(macro):

        @pl.when(my_macro == m)
        def _(m=m):
            for t, (stripe, c) in enumerate(lists[m]):
                low = stripe * unit - m * rows
                held[m, my_pool, t * unit:(t + 1) * unit, :] = panel_ref[
                    0, low:low + unit, c * LANES:(c + 1) * LANES]
            for t, b in enumerate(range(m, blocks, macro)):
                part = loads_ref[:, 0, b * LANES:(b + 1) * LANES]
                part = jnp.concatenate([part, jnp.zeros((PACK - count, LANES), F32)], axis=0)
                low = most * unit + t * PACK
                held[m, my_pool, low:low + PACK, :] = part.astype(BF)

    pl.semaphore_wait(barrier, expected)
    pending = []

    def copy_of(src, h, to, core, sem):
        m, p = src
        start, size = cuts[h]
        view = held.at[m, p, pl.ds(start, size), :]
        return pltpu.make_async_remote_copy(
            src_ref=view, dst_ref=view, send_sem=send_sem.at[sem], recv_sem=recv_sem.at[m, p, h],
            device_id=device(to, core), device_id_type=pl.DeviceIdType.MESH)

    def start(src, h, to, core, cond):
        copy = copy_of(src, h, to, core, len(pending))
        pending.append((copy, cond))
        if cond is None:
            copy.start()
        else:
            pl.when(cond)(copy.start)

    def arrive(src, h):
        copy_of(src, h, here, 1 - pc, 0).wait_recv()

    def along(src, h, axis, k, source):
        n, p = extent[axis], here[axis]
        if n == 1 or (k > 0 and n == 2):
            return
        if k == 0 and n == 2:
            start(src, h, moved(axis, 1 - p), pc, None)
        elif k == 0:
            for by in (1, -1):
                to = p + by
                start(src, h, moved(axis, to), pc, jnp.logical_and(to >= 0, to < n))
        else:
            to = jnp.where(p > source, p + 1, p - 1)
            start(src, h, moved(axis, to), pc, jnp.logical_and(to >= 0, to < n))

    paths = ((0, 1, 2), (0, 2, 1))

    def sources(ks):
        return tuple(here[a] if ks[a] == 0 else pick(orders[a], here[a], ks[a]) for a in range(3))

    def event(ks, h):
        at = sources(ks)
        src = device(at, pc)
        if any(ks):
            arrive(src, h)
        path = paths[h]
        last = max([i for i in range(3) if ks[path[i]]], default=0)
        for i in range(last, 3):
            along(src, h, path[i], ks[path[i]], at[path[i]])
        start(src, h, here, 1 - pc, None)

    def events_z(kz):
        return [functools.partial(event, (kz, 0, 0), h) for h in (0, 1)] if kz < nz else []

    def events_xy(kz):
        if kz >= nz:
            return []
        first = [((kz, k, 0), 0) for k in range(1, nx)] + [((kz, 0, k), 1) for k in range(1, ny)]
        second = [((kz, kx, ky), 0) for kx in range(nx) for ky in range(1, ny)]
        second += [((kz, kx, ky), 1) for ky in range(ny) for kx in range(1, nx)]
        return [functools.partial(event, ks, h) for ks, h in dict.fromkeys(first + second)]

    def run(steps):
        for step in steps:
            step()

    def sibling(kz):
        for kx in range(nx):
            for ky in range(ny):
                at = sources((kz, kx, ky))
                for h in (0, 1):
                    arrive(device(at, 1 - pc), h)

    run(events_z(0))

    _, slot_row = slots_of(family_ref[...], pool)
    placing = (lax.broadcasted_iota(jnp.int32, (slots, points), 0) == slot_row).astype(BF)

    for i in range(count):
        span = slice(i * dof, (i + 1) * dof)
        slot_prev[:, span] = jnp.dot(placing, previous_ref[:, span], preferred_element_type=F32).astype(BF)
    slot_contact[...] = sum(
        jnp.dot(placing, part, preferred_element_type=F32) for part in parts3(contact_ref[...]))
    slot_strain[...] = sum(
        lax.dot_general(placing, part, NT, preferred_element_type=F32) for part in parts3(strain_ref[...]))
    slot_small[...] = jnp.zeros_like(slot_small)

    eye = (lax.broadcasted_iota(jnp.int32, (LANES, LANES), 0)
           == lax.broadcasted_iota(jnp.int32, (LANES, LANES), 1))

    def assemble(j, f):
        for m in range(macro):
            for t, (stripe, c) in enumerate(lists[m]):
                whole[j, stripe * unit:(stripe + 1) * unit, c * LANES:(c + 1) * LANES] = held[
                    m, f, t * unit:(t + 1) * unit, :]
            for t, b in enumerate(range(m, blocks, macro)):
                low = most * unit + t * PACK
                load[j, :, b * LANES:(b + 1) * LANES] = held[m, f, low:low + PACK, :]
        for r, c in mirrored:
            block = whole[j, r * LANES:(r + 1) * LANES, c * LANES:(c + 1) * LANES]
            whole[j, c * LANES:(c + 1) * LANES, r * LANES:(r + 1) * LANES] = block.T
        for r in range(blocks):
            span = slice(r * LANES, (r + 1) * LANES)
            diagonal = jnp.sum(jnp.where(eye, whole[j, span, span].astype(F32), 0.0), axis=0, keepdims=True)
            inverse_ref[j, :, span] = jnp.broadcast_to(1.0 / diagonal, (CAP, LANES))

    def solve_pair(pair, between):
        at16 = pl.ds(pl.multiple_of(pair * 2 * CAP, 2 * CAP), 2 * CAP)
        for j in (0, 1):
            assemble(j, pair * 2 + j)
        for i in range(count):
            both = slot_prev[at16, i * dof:(i + 1) * dof].astype(F32)
            iterate[0, i * CAP:(i + 1) * CAP, :] = both[:CAP]
            iterate[1, i * CAP:(i + 1) * CAP, :] = both[CAP:]

        def contact_of(j):
            return slot_contact[pl.ds(pl.multiple_of(pair * 2 * CAP + j * CAP, CAP), CAP), :]

        cases = [slice(i * CAP, (i + 1) * CAP) for i in range(count)]

        def multiply(field):
            for j in (0, 1):
                product[j] = jnp.dot(field[j].astype(BF), whole[j], preferred_element_type=F32)

        multiply(iterate)
        current = []
        for j in (0, 1):
            extra, inverse = contact_of(j), inverse_ref[j]
            for i, case in enumerate(cases):
                left = load[j, i:i + 1, :].astype(F32) - (product[j, case, :] + extra * iterate[j, case, :])
                scaled = inverse * left
                residual[j, case, :] = left
                direction[j, case, :] = scaled
                current.append(jnp.sum(left * scaled, axis=-1, keepdims=True))

        def sweep(current):
            multiply(direction)
            after = []
            for j in (0, 1):
                extra, inverse = contact_of(j), inverse_ref[j]
                for i, case in enumerate(cases):
                    before = current[j * count + i]
                    toward = direction[j, case, :]
                    image = product[j, case, :] + extra * toward
                    step = before / (jnp.sum(toward * image, axis=-1, keepdims=True) + 1e-6)
                    iterate[j, case, :] = iterate[j, case, :] + step * toward
                    left = residual[j, case, :] - step * image
                    scaled = inverse * left
                    updated = jnp.sum(left * scaled, axis=-1, keepdims=True)
                    residual[j, case, :] = left
                    direction[j, case, :] = scaled + (updated / (before + 1e-6)) * toward
                    after.append(updated)
            return after

        between()
        for _ in range(ITERS):
            current = sweep(current)
            between()

        for i in range(count):
            span = slice(i * CAP, (i + 1) * CAP)
            both = jnp.concatenate([iterate[0, span, :], iterate[1, span, :]], axis=0)
            slot_out[at16, i * dof:(i + 1) * dof] = both.astype(BF)
        for j in (0, 1):
            mine = pl.ds(pl.multiple_of(pair * 2 * CAP + j * CAP, CAP), CAP)
            value = iterate[j]
            high = value.astype(BF)
            low = (value - high.astype(F32)).astype(BF)
            weights = load[j]
            tang = (lax.dot_general(high, weights, NT, preferred_element_type=F32)
                    + lax.dot_general(low, weights, NT, preferred_element_type=F32)) * (1.0 / dof)
            strain = slot_strain[mine, :]
            for i in range(count):
                piece = tang[i * CAP:(i + 1) * CAP, 0:count]
                slot_small[mine, i * count:(i + 1) * count] = piece
                slot_small[mine, count * count + i:count * count + i + 1] = jnp.sum(
                    piece * strain, axis=-1, keepdims=True)

    def solve(kz, steps):
        at = pick(orders[0], pz, kz) if kz else pz
        share = -(-len(steps) // (ITERS + 1))

        def between():
            run(steps[:share])
            del steps[:share]

        for q in range(nx // 2):
            solve_pair(at * (nx // 2) + q, between)

    run(events_z(1) + events_xy(0) + events_z(2))
    for kz in range(nz):
        sibling(kz)
        solve(kz, events_z(kz + 3) + events_xy(kz + 1))

    for copy, cond in pending:
        if cond is None:
            copy.wait_send()
        else:
            pl.when(cond)(copy.wait_send)


def count_sends(nz, nx, ny):
    def along(n, k):
        if n == 1 or (k > 0 and n == 2):
            return 0
        return 1 if n == 2 or k > 0 else 2

    total = 0
    for path in ((0, 1, 2), (0, 2, 1)):
        for ks in itertools.product(range(nz), range(nx), range(ny)):
            last = max([i for i in range(3) if ks[path[i]]], default=0)
            total += 1 + sum(along((nz, nx, ny)[path[i]], ks[path[i]]) for i in range(last, 3))
    return total


def on_device(macro, pool, panels, loads, family, contact, strain, previous):
    points, dof = contact.shape
    count = strain.shape[1]
    plan = half_plan(dof, macro)
    unit, most = plan[0], plan[1]
    shares = -(-(dof // LANES) // macro)
    total_rows = most * unit + shares * PACK
    cut = -(-total_rows // (2 * PACK)) * PACK
    slots = pool * CAP
    nz, nx = split_pool(pool)
    vmem = pl.BlockSpec(memory_space=pltpu.VMEM)
    family_row = family.T
    slot_out, slot_small = pl.pallas_call(
        functools.partial(kernel, (macro, pool, plan, cut)),
        out_shape=(
            jax.ShapeDtypeStruct((slots, count * dof), BF),
            jax.ShapeDtypeStruct((slots, LANES), F32),
        ),
        in_specs=[vmem] * 6,
        out_specs=(vmem,) * 2,
        scratch_shapes=[
            pltpu.VMEM((macro, pool, total_rows, LANES), BF),
            pltpu.VMEM((2, dof, dof), BF),
            pltpu.VMEM((2, PACK, dof), BF),
            pltpu.VMEM((slots, count * dof), BF),
            pltpu.VMEM((slots, dof), F32),
            pltpu.VMEM((slots, count), F32),
            pltpu.VMEM((2, count * CAP, dof), F32),
            pltpu.VMEM((2, count * CAP, dof), F32),
            pltpu.VMEM((2, count * CAP, dof), F32),
            pltpu.VMEM((2, count * CAP, dof), F32),
            pltpu.VMEM((2, CAP, dof), F32),
            pltpu.SemaphoreType.DMA((count_sends(nz, nx, macro // CORES),)),
            pltpu.SemaphoreType.DMA((macro, pool, 2)),
        ],
        compiler_params=pltpu.CompilerParams(
            collective_id=0, has_side_effects=True, vmem_limit_bytes=56 * 1024 * 1024),
    )(panels, loads.transpose(1, 0, 2), family_row, contact, strain.T, previous)
    fluct, stress, tangent = pl.pallas_call(
        functools.partial(unplace_kernel, pool, count),
        out_shape=(
            jax.ShapeDtypeStruct(previous.shape, BF),
            jax.ShapeDtypeStruct((count, points), F32),
            jax.ShapeDtypeStruct((points, count * count), F32),
        ),
        in_specs=[vmem] * 3,
        out_specs=(vmem,) * 3,
        compiler_params=pltpu.CompilerParams(vmem_limit_bytes=32 * 1024 * 1024),
    )(family_row, slot_out, slot_small)
    return fluct, stress.T, tangent


def solution(mesh):
    placed = (
        P("pool", "macro", None),
        P("pool", None, None),
        P(("macro", "pool"), None),
        P(("macro", "pool"), None),
        P(("macro", "pool"), None),
        P(("macro", "pool"), None),
    )
    return jax.shard_map(
        functools.partial(on_device, mesh.shape["macro"], mesh.shape["pool"]),
        mesh=mesh,
        in_specs=placed,
        out_specs=(
            P(("macro", "pool"), None),
            P(("macro", "pool"), None),
            P(("macro", "pool"), None),
        ),
        check_vma=False,
    )
```

```python
import functools
import itertools
import math

import jax
import jax.numpy as jnp
from jax import lax
from jax.experimental import pallas as pl
from jax.experimental.pallas import tpu as pltpu
from jax.sharding import PartitionSpec as P

ITERS = 4
CAP = 8
LANES = 128
PACK = 16
CORES = 2
BF = jnp.bfloat16
F32 = jnp.float32


def split_pool(pool):
    fast = max(d for d in range(1, pool + 1) if pool % d == 0 and d * d <= pool)
    return pool // fast, fast


def half_plan(dof, macro):
    rows = dof // macro
    unit = math.gcd(rows, LANES)
    blocks = dof // LANES
    per = LANES // unit
    fixed = [(r, (r + k) % blocks) for r in range(blocks) for k in range((blocks - 1) // 2 + 1)]
    open_pairs = [(r, r + blocks // 2) for r in range(blocks // 2)] if blocks % 2 == 0 else []
    best = None
    for turned in itertools.product((0, 1), repeat=len(open_pairs)):
        chosen = fixed + [(b, a) if t else (a, b) for t, (a, b) in zip(turned, open_pairs)]
        lists = [[] for _ in range(macro)]
        for r, c in sorted(chosen):
            for q in range(per):
                stripe = r * per + q
                lists[stripe * unit // rows].append((stripe, c))
        most = max(len(each) for each in lists)
        if best is None or most < best[0]:
            best = (most, lists, chosen)
    return unit, best[0], best[1], [(r, c) for r, c in best[2] if r != c]


def by_distance(n):
    return [sorted(range(n), key=lambda s: (abs(s - p), s)) for p in range(n)]


def pick(table, at, k):
    out = jnp.int32(table[0][k])
    for p in range(1, len(table)):
        out = jnp.where(at == p, jnp.int32(table[p][k]), out)
    return out


PATHS = ((0, 1, 2), (0, 2, 1), (1, 2, 0))
NT = (((1,), (1,)), ((), ()))


def parts3(value):
    high = value.astype(BF)
    rest = value - high.astype(F32)
    middle = rest.astype(BF)
    return high, middle, (rest - middle.astype(F32)).astype(BF)


def slots_of(family_row, pool):
    points = family_row.shape[1]
    row_at = lax.broadcasted_iota(jnp.int32, (points, points), 0)
    col_at = lax.broadcasted_iota(jnp.int32, (points, points), 1)
    eye = row_at == col_at
    wide = jnp.broadcast_to(family_row.astype(F32), (points, points))
    family = jnp.sum(jnp.where(eye, wide, 0.0), axis=1, keepdims=True).astype(jnp.int32)
    earlier = jnp.logical_and(wide.astype(jnp.int32) == family, col_at < row_at)
    rank = jnp.sum(jnp.where(earlier, 1.0, 0.0), axis=1, keepdims=True)
    slot = family * CAP + rank.astype(jnp.int32)
    slot_row = jnp.sum(jnp.where(eye, slot.astype(F32), 0.0), axis=0, keepdims=True).astype(jnp.int32)
    return slot, slot_row


def unplace_kernel(pool, count, family_ref, out_ref, small_ref, fluct_ref, stress_ref, tangent_ref):
    points = family_ref.shape[1]
    slot, _ = slots_of(family_ref[...], pool)
    taking = (slot == lax.broadcasted_iota(jnp.int32, (points, pool * CAP), 1)).astype(BF)
    fluct_ref[...] = jnp.dot(taking, out_ref[...], preferred_element_type=F32).astype(BF)
    small = sum(jnp.dot(taking, part, preferred_element_type=F32) for part in parts3(small_ref[...]))
    tangent_ref[...] = small[:, 0:count * count]
    at = lax.broadcasted_iota(jnp.int32, (PACK, LANES), 0) + count * count
    picking = (at == lax.broadcasted_iota(jnp.int32, (PACK, LANES), 1)).astype(BF)
    turned = sum(lax.dot_general(picking, part, NT, preferred_element_type=F32) for part in parts3(small))
    stress_ref[...] = turned[0:count, :]


def kernel(sizes, panel_ref, loads_ref, family_ref, contact_ref, strain_ref, previous_ref,
           slot_out, slot_small,
           held, whole, load, slot_prev, slot_contact, slot_strain,
           iterate, residual, direction, product, inverse_ref, send_sem, recv_sem):
    macro, pool, plan, cut = sizes
    unit, most, lists, mirrored = plan
    count, dof = loads_ref.shape[0], loads_ref.shape[2]
    rows = panel_ref.shape[1]
    points = family_ref.shape[1]
    slots = pool * CAP
    blocks = dof // LANES
    nz, nx = split_pool(pool)
    ny = macro // CORES
    total_rows = held.shape[2]
    cuts = ((0, cut[0]), (cut[0], cut[1] - cut[0]), (cut[1], total_rows - cut[1]))

    my_macro, my_pool = lax.axis_index("macro"), lax.axis_index("pool")
    pz, px = my_pool // nx, my_pool % nx
    py, pc = my_macro // CORES, my_macro % CORES
    here = (pz, px, py)
    extent = (nz, nx, ny)
    orders = tuple(by_distance(n) for n in extent)

    def device(at, core):
        z, x, y = at
        return (y * CORES + core, z * nx + x)

    def moved(axis, to):
        return tuple(to if a == axis else here[a] for a in range(3))

    barrier = pltpu.get_barrier_semaphore()
    pl.semaphore_signal(barrier, inc=1, device_id=device(here, 1 - pc), device_id_type=pl.DeviceIdType.MESH)
    expected = jnp.int32(1)
    for axis in range(3):
        for by in (-1, 1):
            to = here[axis] + by
            ok = jnp.logical_and(to >= 0, to < extent[axis])
            expected = expected + ok.astype(jnp.int32)

            @pl.when(ok)
            def _(axis=axis, to=to):
                pl.semaphore_signal(
                    barrier, inc=1, device_id=device(moved(axis, to), pc), device_id_type=pl.DeviceIdType.MESH)

    for m in range(macro):

        @pl.when(my_macro == m)
        def _(m=m):
            for t, (stripe, c) in enumerate(lists[m]):
                low = stripe * unit - m * rows
                held[m, my_pool, t * unit:(t + 1) * unit, :] = panel_ref[
                    0, low:low + unit, c * LANES:(c + 1) * LANES]
            for t, b in enumerate(range(m, blocks, macro)):
                part = loads_ref[:, 0, b * LANES:(b + 1) * LANES]
                part = jnp.concatenate([part, jnp.zeros((PACK - count, LANES), F32)], axis=0)
                low = most * unit + t * PACK
                held[m, my_pool, low:low + PACK, :] = part.astype(BF)

    pl.semaphore_wait(barrier, expected)
    pending = []

    def copy_of(src, h, to, core, sem):
        m, p = src
        start, size = cuts[h]
        view = held.at[m, p, pl.ds(start, size), :]
        return pltpu.make_async_remote_copy(
            src_ref=view, dst_ref=view, send_sem=send_sem.at[sem], recv_sem=recv_sem.at[m, p, h],
            device_id=device(to, core), device_id_type=pl.DeviceIdType.MESH)

    def start(src, h, to, core, cond):
        copy = copy_of(src, h, to, core, len(pending))
        pending.append((copy, cond))
        if cond is None:
            copy.start()
        else:
            pl.when(cond)(copy.start)

    def arrive(src, h):
        copy_of(src, h, here, 1 - pc, 0).wait_recv()

    def along(src, h, axis, k, source):
        n, p = extent[axis], here[axis]
        if n == 1 or (k > 0 and n == 2):
            return
        if k == 0 and n == 2:
            start(src, h, moved(axis, 1 - p), pc, None)
        elif k == 0:
            for by in (1, -1):
                to = p + by
                start(src, h, moved(axis, to), pc, jnp.logical_and(to >= 0, to < n))
        else:
            to = jnp.where(p > source, p + 1, p - 1)
            start(src, h, moved(axis, to), pc, jnp.logical_and(to >= 0, to < n))


    def sources(ks):
        return tuple(here[a] if ks[a] == 0 else pick(orders[a], here[a], ks[a]) for a in range(3))

    def event(ks, h):
        at = sources(ks)
        src = device(at, pc)
        if any(ks):
            arrive(src, h)
        path = PATHS[h]
        last = max([i for i in range(3) if ks[path[i]]], default=0)
        for i in range(last, 3):
            along(src, h, path[i], ks[path[i]], at[path[i]])
        start(src, h, here, 1 - pc, None)

    def events_z(kz):
        return [functools.partial(event, (kz, 0, 0), h) for h in (0, 1)] if kz < nz else []

    def events_xy(kz):
        if kz >= nz:
            return []
        first = [((kz, k, 0), 0) for k in range(1, nx)] + [((kz, 0, k), 1) for k in range(1, ny)]
        second = [((kz, kx, ky), 0) for kx in range(nx) for ky in range(1, ny)]
        second += [((kz, kx, ky), 1) for ky in range(ny) for kx in range(1, nx)]
        return [functools.partial(event, ks, h) for ks, h in dict.fromkeys(first + second)]

    def events_last(kz):
        if kz >= nz:
            return []
        first = [(kz, k, 0) for k in range(0 if kz else 1, nx)]
        second = [(kz, kx, ky) for kx in range(nx) for ky in range(1, ny)]
        return [functools.partial(event, ks, 2) for ks in first + second]

    def run(steps):
        for step in steps:
            step()

    def sibling(kz):
        for kx in range(nx):
            for ky in range(ny):
                at = sources((kz, kx, ky))
                for h in range(len(PATHS)):
                    arrive(device(at, 1 - pc), h)

    run(events_z(0))
    event((0, 0, 0), 2)

    _, slot_row = slots_of(family_ref[...], pool)
    placing = (lax.broadcasted_iota(jnp.int32, (slots, points), 0) == slot_row).astype(BF)

    for i in range(count):
        span = slice(i * dof, (i + 1) * dof)
        slot_prev[:, span] = jnp.dot(placing, previous_ref[:, span], preferred_element_type=F32).astype(BF)
    slot_contact[...] = sum(
        jnp.dot(placing, part, preferred_element_type=F32) for part in parts3(contact_ref[...]))
    slot_strain[...] = sum(
        lax.dot_general(placing, part, NT, preferred_element_type=F32) for part in parts3(strain_ref[...]))
    slot_small[...] = jnp.zeros_like(slot_small)

    eye = (lax.broadcasted_iota(jnp.int32, (LANES, LANES), 0)
           == lax.broadcasted_iota(jnp.int32, (LANES, LANES), 1))

    def assemble(j, f):
        for m in range(macro):
            for t, (stripe, c) in enumerate(lists[m]):
                whole[j, stripe * unit:(stripe + 1) * unit, c * LANES:(c + 1) * LANES] = held[
                    m, f, t * unit:(t + 1) * unit, :]
            for t, b in enumerate(range(m, blocks, macro)):
                low = most * unit + t * PACK
                load[j, :, b * LANES:(b + 1) * LANES] = held[m, f, low:low + PACK, :]
        for r, c in mirrored:
            block = whole[j, r * LANES:(r + 1) * LANES, c * LANES:(c + 1) * LANES]
            whole[j, c * LANES:(c + 1) * LANES, r * LANES:(r + 1) * LANES] = block.T
        for r in range(blocks):
            span = slice(r * LANES, (r + 1) * LANES)
            diagonal = jnp.sum(jnp.where(eye, whole[j, span, span].astype(F32), 0.0), axis=0, keepdims=True)
            inverse_ref[j, :, span] = jnp.broadcast_to(1.0 / diagonal, (CAP, LANES))

    def solve_pair(pair, between):
        at16 = pl.ds(pl.multiple_of(pair * 2 * CAP, 2 * CAP), 2 * CAP)
        for j in (0, 1):
            assemble(j, pair * 2 + j)
        for i in range(count):
            both = slot_prev[at16, i * dof:(i + 1) * dof].astype(F32)
            iterate[0, i * CAP:(i + 1) * CAP, :] = both[:CAP]
            iterate[1, i * CAP:(i + 1) * CAP, :] = both[CAP:]

        def contact_of(j):
            return slot_contact[pl.ds(pl.multiple_of(pair * 2 * CAP + j * CAP, CAP), CAP), :]

        cases = [slice(i * CAP, (i + 1) * CAP) for i in range(count)]

        def multiply(field):
            for j in (0, 1):
                product[j] = jnp.dot(field[j].astype(BF), whole[j], preferred_element_type=F32)

        multiply(iterate)
        current = []
        for j in (0, 1):
            extra, inverse = contact_of(j), inverse_ref[j]
            for i, case in enumerate(cases):
                left = load[j, i:i + 1, :].astype(F32) - (product[j, case, :] + extra * iterate[j, case, :])
                scaled = inverse * left
                residual[j, case, :] = left
                direction[j, case, :] = scaled
                current.append(jnp.sum(left * scaled, axis=-1, keepdims=True))

        def sweep(current):
            multiply(direction)
            after = []
            for j in (0, 1):
                extra, inverse = contact_of(j), inverse_ref[j]
                for i, case in enumerate(cases):
                    before = current[j * count + i]
                    toward = direction[j, case, :]
                    image = product[j, case, :] + extra * toward
                    step = before / (jnp.sum(toward * image, axis=-1, keepdims=True) + 1e-6)
                    iterate[j, case, :] = iterate[j, case, :] + step * toward
                    left = residual[j, case, :] - step * image
                    scaled = inverse * left
                    updated = jnp.sum(left * scaled, axis=-1, keepdims=True)
                    residual[j, case, :] = left
                    direction[j, case, :] = scaled + (updated / (before + 1e-6)) * toward
                    after.append(updated)
            return after

        between()
        for _ in range(ITERS):
            current = sweep(current)
            between()

        for i in range(count):
            span = slice(i * CAP, (i + 1) * CAP)
            both = jnp.concatenate([iterate[0, span, :], iterate[1, span, :]], axis=0)
            slot_out[at16, i * dof:(i + 1) * dof] = both.astype(BF)
        for j in (0, 1):
            mine = pl.ds(pl.multiple_of(pair * 2 * CAP + j * CAP, CAP), CAP)
            value = iterate[j]
            high = value.astype(BF)
            low = (value - high.astype(F32)).astype(BF)
            weights = load[j]
            tang = (lax.dot_general(high, weights, NT, preferred_element_type=F32)
                    + lax.dot_general(low, weights, NT, preferred_element_type=F32)) * (1.0 / dof)
            strain = slot_strain[mine, :]
            for i in range(count):
                piece = tang[i * CAP:(i + 1) * CAP, 0:count]
                slot_small[mine, i * count:(i + 1) * count] = piece
                slot_small[mine, count * count + i:count * count + i + 1] = jnp.sum(
                    piece * strain, axis=-1, keepdims=True)

    def solve(kz, steps):
        at = pick(orders[0], pz, kz) if kz else pz
        share = -(-len(steps) // (ITERS + 1))

        def between():
            run(steps[:share])
            del steps[:share]

        for q in range(nx // 2):
            solve_pair(at * (nx // 2) + q, between)

    run(events_z(1) + events_xy(0) + events_last(0) + events_z(2) + events_last(1))
    for kz in range(nz):
        sibling(kz)
        solve(kz, events_z(kz + 3) + events_xy(kz + 1) + events_last(kz + 2))

    for copy, cond in pending:
        if cond is None:
            copy.wait_send()
        else:
            pl.when(cond)(copy.wait_send)


def count_sends(nz, nx, ny):
    def along(n, k):
        if n == 1 or (k > 0 and n == 2):
            return 0
        return 1 if n == 2 or k > 0 else 2

    total = 0
    for path in PATHS:
        for ks in itertools.product(range(nz), range(nx), range(ny)):
            last = max([i for i in range(3) if ks[path[i]]], default=0)
            total += 1 + sum(along((nz, nx, ny)[path[i]], ks[path[i]]) for i in range(last, 3))
    return total


def on_device(macro, pool, panels, loads, family, contact, strain, previous):
    points, dof = contact.shape
    count = strain.shape[1]
    plan = half_plan(dof, macro)
    unit, most = plan[0], plan[1]
    shares = -(-(dof // LANES) // macro)
    total_rows = most * unit + shares * PACK
    last = (2 * total_rows // 9 + PACK // 2) // PACK * PACK
    first = -(-(total_rows - last) // (2 * PACK)) * PACK
    cut = (first, total_rows - last)
    slots = pool * CAP
    nz, nx = split_pool(pool)
    vmem = pl.BlockSpec(memory_space=pltpu.VMEM)
    family_row = family.T
    slot_out, slot_small = pl.pallas_call(
        functools.partial(kernel, (macro, pool, plan, cut)),
        out_shape=(
            jax.ShapeDtypeStruct((slots, count * dof), BF),
            jax.ShapeDtypeStruct((slots, LANES), F32),
        ),
        in_specs=[vmem] * 6,
        out_specs=(vmem,) * 2,
        scratch_shapes=[
            pltpu.VMEM((macro, pool, total_rows, LANES), BF),
            pltpu.VMEM((2, dof, dof), BF),
            pltpu.VMEM((2, PACK, dof), BF),
            pltpu.VMEM((slots, count * dof), BF),
            pltpu.VMEM((slots, dof), F32),
            pltpu.VMEM((slots, count), F32),
            pltpu.VMEM((2, count * CAP, dof), F32),
            pltpu.VMEM((2, count * CAP, dof), F32),
            pltpu.VMEM((2, count * CAP, dof), F32),
            pltpu.VMEM((2, count * CAP, dof), F32),
            pltpu.VMEM((2, CAP, dof), F32),
            pltpu.SemaphoreType.DMA((count_sends(nz, nx, macro // CORES),)),
            pltpu.SemaphoreType.DMA((macro, pool, len(PATHS))),
        ],
        compiler_params=pltpu.CompilerParams(
            collective_id=0, has_side_effects=True, vmem_limit_bytes=56 * 1024 * 1024),
    )(panels, loads.transpose(1, 0, 2), family_row, contact, strain.T, previous)
    fluct, stress, tangent = pl.pallas_call(
        functools.partial(unplace_kernel, pool, count),
        out_shape=(
            jax.ShapeDtypeStruct(previous.shape, BF),
            jax.ShapeDtypeStruct((count, points), F32),
            jax.ShapeDtypeStruct((points, count * count), F32),
        ),
        in_specs=[vmem] * 3,
        out_specs=(vmem,) * 3,
        compiler_params=pltpu.CompilerParams(vmem_limit_bytes=56 * 1024 * 1024),
    )(family_row, slot_out, slot_small)
    return fluct, stress.T, tangent


def solution(mesh):
    placed = (
        P("pool", "macro", None),
        P("pool", None, None),
        P(("macro", "pool"), None),
        P(("macro", "pool"), None),
        P(("macro", "pool"), None),
        P(("macro", "pool"), None),
    )
    return jax.shard_map(
        functools.partial(on_device, mesh.shape["macro"], mesh.shape["pool"]),
        mesh=mesh,
        in_specs=placed,
        out_specs=(
            P(("macro", "pool"), None),
            P(("macro", "pool"), None),
            P(("macro", "pool"), None),
        ),
        check_vma=False,
    )
```
